32 devices in a mesh: gx: 8 (over y, x, core), gy: 4 (over z).
Axes of the slice: x: 2, y: 2, z: 4, core: 2. Of those that a mesh axis runs over, the one named last changes fastest.
Arguments:
- field: float32 [128, 128, 1536], P('gx', 'gy'), may hold values from -24 to 24
- kappa: float32 [128, 128, 1536], P('gx', 'gy'), may hold values from 0.02 to 0.16
- history: float32 [126, 64, 32, 128], P(None, 'gx', 'gy'), may hold values from -2400 to 2400
Outputs:
- field_next: float32 [128, 128, 1536], P('gx', 'gy')
- basis: float32 [128, 64, 32, 128], P(None, 'gx', 'gy')
- factor: float32 [128, 128], replicated
The draws below stay inside these ranges and needn't reach their ends.
All inputs are finite; a program needn't handle non-finite values.
Results may differ from the reference program's by a relative error of at most 0.00018.
Values sent between devices are 32-bit elements; how exact they have to be, the bound alone decides.
A program may use at most 192 MiB of HBM per device.

```python
import math
import jax
import jax.numpy as jnp
from jax import lax

NZ = 1536
PAST = 126
NX = 128
NY = 128
NXS = 64
NYS = 32
NZS = 128


def draw_history(key, part):
    key_a, key_b = jax.random.split(key, 2)
    shape = (PAST, NXS, NYS, NZS)
    across = jnp.arange(NXS, dtype=jnp.float32) / max(NXS - 1, 1)
    row_scale = 10.0 ** across
    col_scale = 10.0 ** jax.random.uniform(key_b, (PAST,), jnp.float32)
    base = jnp.clip(jax.random.normal(key_a, shape, jnp.float32), -6.0, 6.0)
    scales = row_scale[:, None] * jnp.ones((NYS,), jnp.float32)[None, :]
    out = base * col_scale[:, None, None, None] * scales[None, :, :, None]
    return out.astype(jnp.float32)


def levels(rng, dims, cuts, smallest, high):
    factor_of = 1.0
    for axis_at, blocks in cuts:
        heights = jax.random.uniform(jax.random.fold_in(jax.random.fold_in(rng, 6), axis_at), (blocks,), jnp.float32, smallest / len(cuts), high / len(cuts))
        factor_of = factor_of * jnp.repeat(jnp.exp(heights), dims[axis_at] // blocks).reshape((-1,) + (1,) * (len(dims) - 1 - axis_at))
    return factor_of


def gaussian(key, extent, width, bound, cuts=(), kind=jnp.bfloat16):
    result = jax.random.normal(key, extent, jnp.float32) * width
    if len(cuts) > 0:
        result = levels(key, extent, cuts, -0.22, 0.18) * result
    return jnp.clip(result, min=-bound, max=bound).astype(kind)


def setup_inputs(seed: int = 0) -> dict:
    key_of = jax.random.split(jax.random.key(seed), 4)
    field = gaussian(key_of[0], (NX, NY, NZ), 4.0, 24.0, ((0, 8), (1, 4)), jnp.float32)
    kappa = jnp.clip(jnp.exp(math.log(0.16) - 2.0794415 * jax.random.uniform(key_of[1], (NX, NY, NZ), jnp.float32) ** levels(key_of[1], (NX, NY, NZ), ((0, 8), (1, 4)), -0.2, 0.2)), 0.02, 0.16)
    history = draw_history(jax.random.fold_in(key_of[3], 71), 0)
    return dict(field=field, kappa=kappa, history=history)


def advance(field_pad, kappa_pad):
    field_z = jnp.pad(field_pad, ((0, 0), (0, 0), (1, 1)))
    kappa_z = jnp.pad(kappa_pad, ((0, 0), (0, 0), (1, 1)))
    centre = field_z[1:-1, 1:-1, 1:-1]
    kcentre = kappa_z[1:-1, 1:-1, 1:-1]
    places = [(slice(2, None), slice(1, -1), slice(1, -1)), (slice(None, -2), slice(1, -1), slice(1, -1)), (slice(1, -1), slice(2, None), slice(1, -1)), (slice(1, -1), slice(None, -2), slice(1, -1)), (slice(1, -1), slice(1, -1), slice(2, None)), (slice(1, -1), slice(1, -1), slice(None, -2))]
    change = jnp.zeros_like(centre)
    for place in places:
        change = change + 0.5 * (kcentre + kappa_z[place]) * (field_z[place] - centre)
    return centre + change

def sample(field):
    a, b, c = field.shape
    return field.reshape(a // 2, 2, b // 4, 4, c // 12, 12)[:, 0, :, 0, :, 0]

def reference(field, kappa, history):
    kappa_pad = jnp.pad(kappa, ((1, 1), (1, 1), (0, 0)))
    first = advance(jnp.pad(field, ((1, 1), (1, 1), (0, 0))), kappa_pad)
    second = advance(jnp.pad(first, ((1, 1), (1, 1), (0, 0))), kappa_pad)
    block = jnp.concatenate([history, sample(first)[None], sample(second)[None]], 0)
    shape = block.shape
    block = block.reshape(shape[0], -1)
    gram = jnp.einsum('ar,br->ab', block, block, precision=lax.Precision.HIGHEST) / block.shape[1]
    factor = jnp.linalg.cholesky(gram).T
    basis = lax.linalg.triangular_solve(factor.T, block, left_side=True, lower=True)
    return (second, basis.reshape(shape), factor)
```

```python
import functools

import jax
import jax.numpy as jnp
from jax import lax
from jax.experimental import pallas as pl
from jax.experimental.pallas import tpu as pltpu
from jax.sharding import PartitionSpec as P

F32 = jnp.float32
BF16 = jnp.bfloat16
TOP = 8
MESH = pl.DeviceIdType.MESH


def dot(a, b, contract):
    return lax.dot_general(
        a, b, ((contract[:1], contract[1:]), ((), ())), preferred_element_type=F32
    )


def split(x):
    hi = x.astype(BF16)
    return hi, (x - hi.astype(F32)).astype(BF16)


def stencil(v, k, out, tiles):
    size_x = v.shape[0] - 2
    depth = v.shape[2]
    lane = lax.broadcasted_iota(jnp.int32, (8, depth), 1)

    for tile in tiles:
        at = TOP + 8 * tile
        rows = pl.ds(at, 8)
        up = pl.ds(at + 1, 8)
        down = pl.ds(at - 1, 8)

        def layer(x, flux):
            c, kc = v[x, rows, :], k[x, rows, :]
            ahead = (kc + k[x + 1, rows, :]) * (v[x + 1, rows, :] - c)
            acc = ahead - flux
            acc += (kc + k[x, up, :]) * (v[x, up, :] - c)
            acc += (kc + k[x, down, :]) * (v[x, down, :] - c)
            last = lane == depth - 1
            c_up = jnp.where(last, 0.0, pltpu.roll(c, depth - 1, 1))
            k_up = jnp.where(last, 0.0, pltpu.roll(kc, depth - 1, 1))
            face = (kc + k_up) * (c_up - c)
            acc += face
            acc -= jnp.where(lane == 0, kc * c, pltpu.roll(face, 1, 1))
            out[x, rows, :] = c + 0.5 * acc
            return ahead

        first = (k[0, rows, :] + k[1, rows, :]) * (v[1, rows, :] - v[0, rows, :])
        lax.fori_loop(1, size_x + 1, layer, first)


def sample(v, pick, rows_y):
    parts = []
    for x in range(1, v.shape[0] - 1, 2):
        parts += [v[x, pl.ds(TOP + 4 * y, 1), :] for y in range(rows_y)]
    x = jnp.concatenate(parts, axis=0)
    hi = x.astype(BF16)
    rest = x - hi.astype(F32)
    mid = rest.astype(BF16)
    low = (rest - mid.astype(F32)).astype(BF16)
    n = x.shape[0]
    got = dot(jnp.concatenate([hi, mid, low], axis=0), pick, (1, 0))
    return got[:n] + got[n : 2 * n] + got[2 * n :]


def evolve(
    nx, ny, past, field, kappa, hist, second_o, s_o, gram_o,
    f, k, v, block, s, gram, slots, red, total, load, halo_send, halo_recv, rs_send, rs_recv, ag_send, ag_recv,
):
    size_x, size_y, depth = field.shape
    gx, gy = lax.axis_index("gx"), lax.axis_index("gy")
    devices = nx * ny
    snaps = gram.shape[0]
    owners = snaps // 8
    step = devices // owners
    me = gy * nx + gx

    def device(flat):
        return (lax.rem(flat, nx), lax.div(flat, nx))

    barrier = pltpu.get_barrier_semaphore()

    def greet(i, carry):
        pl.semaphore_signal(barrier, inc=1, device_id=device(lax.rem(me + i, devices)), device_id_type=MESH)
        return carry

    lax.fori_loop(1, devices, greet, 0)

    inner = (pl.ds(1, size_x), pl.ds(TOP, size_y))
    loads = [
        pltpu.make_async_copy(field, f.at[inner], load.at[0]),
        pltpu.make_async_copy(kappa, k.at[inner], load.at[1]),
        pltpu.make_async_copy(hist, block.at[pl.ds(0, hist.shape[0])], load.at[2]),
    ]
    for copy in loads:
        copy.start()

    left, right = gx > 0, gx < nx - 1
    below, above = gy > 0, gy < ny - 1
    whole_y = pl.ds(TOP, size_y)
    whole_x = pl.ds(1, size_x)
    sides = [
        (left, right, (gx - 1, gy), (1, whole_y), (size_x + 1, whole_y)),
        (right, left, (gx + 1, gy), (size_x, whole_y), (0, whole_y)),
        (below, above, (gx, gy - 1), (whole_x, pl.ds(TOP, 1)), (whole_x, pl.ds(TOP + size_y, 1))),
        (above, below, (gx, gy + 1), (whole_x, pl.ds(TOP + size_y - 1, 1)), (whole_x, pl.ds(TOP - 1, 1))),
    ]

    def halo(ref, which, side):
        to, _, place, src, dst = sides[side]
        return pltpu.make_async_remote_copy(
            src_ref=ref.at[src], dst_ref=ref.at[dst],
            send_sem=halo_send.at[which, side], recv_sem=halo_recv.at[which, side],
            device_id=place, device_id_type=MESH,
        )

    def exchange(ref, which, order):
        for side in order:
            pl.when(sides[side][0])(halo(ref, which, side).start)

    def arrive(ref, which):
        for side in range(4):
            pl.when(sides[side][1])(halo(ref, which, side).wait_recv)

    def sent(ref, which):
        for side in range(4):
            pl.when(sides[side][0])(halo(ref, which, side).wait_send)

    for ref in (f, k, v):
        for side in range(4):
            dst = sides[side][4]

            @pl.when(jnp.logical_not(sides[side][1]))
            def _(ref=ref, dst=dst, side=side):
                if side < 2:
                    ref[dst[0], dst[1], :] = jnp.zeros((size_y, depth), F32)
                else:
                    for x in range(size_x):
                        ref[x + 1, dst[1], :] = jnp.zeros((1, depth), F32)

    pl.semaphore_wait(barrier, devices - 1)
    loads[0].wait()
    exchange(f, 0, range(4))
    loads[1].wait()
    exchange(k, 1, range(4))

    samples = depth // 12
    pick = (
        lax.broadcasted_iota(jnp.int32, (depth, samples), 0)
        == 12 * lax.broadcasted_iota(jnp.int32, (depth, samples), 1)
    ).astype(F32).astype(BF16)

    arrive(f, 0)
    arrive(k, 1)
    tiles = size_y // 8
    edge = sorted({0, tiles - 1})
    middle = [t for t in range(tiles) if t not in edge]
    stencil(f, k, v, edge)
    exchange(v, 2, (2, 3))
    stencil(f, k, v, middle)
    exchange(v, 2, (0, 1))

    loads[2].wait()
    cells = hist.shape[0] // past
    block[pl.ds(past * cells, cells), :] = sample(v, pick, size_y // 4)
    sent(f, 0)
    sent(k, 1)
    arrive(v, 2)
    stencil(v, k, f, range(tiles))
    out = pltpu.make_async_copy(f.at[inner], second_o, load.at[0])
    out.start()
    block[pl.ds((past + 1) * cells, cells), :] = sample(f, pick, size_y // 4)
    sent(v, 2)

    def pair(p, acc):
        x = jnp.concatenate(
            [block[pl.ds(2 * p, snaps, stride=cells), :], block[pl.ds(2 * p + 1, snaps, stride=cells), :]], axis=1
        )
        both = jnp.concatenate(split(x), axis=0)
        s[p] = both
        return acc + dot(both, both, (1, 1))

    acc = lax.fori_loop(0, cells // 2, pair, jnp.zeros((2 * snaps, 2 * snaps), F32))
    gram[...] = (acc[:snaps, :snaps] + acc[snaps:, snaps:]) + (acc[:snaps, snaps:] + acc[snaps:, :snaps])
    keep = pltpu.make_async_copy(s, s_o, load.at[1])
    keep.start()

    is_owner = lax.rem(me, step) == 0
    mine = lax.div(me, step)

    def scatter(j):
        return pltpu.make_async_remote_copy(
            src_ref=gram.at[pl.ds(8 * j, 8)], dst_ref=slots.at[me],
            send_sem=rs_send.at[j], recv_sem=rs_recv.at[me],
            device_id=device(j * step), device_id_type=MESH,
        )

    def start_scatter(j, carry):
        pl.when(j * step != me)(lambda: scatter(j).start())
        return carry

    def end_scatter(j, carry):
        pl.when(j * step != me)(lambda: scatter(j).wait_send())
        return carry

    lax.fori_loop(0, owners, start_scatter, 0)

    def gather(i):
        to = lax.rem(me + i, devices)
        return pltpu.make_async_remote_copy(
            src_ref=red, dst_ref=total.at[pl.ds(8 * mine, 8)],
            send_sem=ag_send.at[i], recv_sem=ag_recv.at[mine],
            device_id=device(to), device_id_type=MESH,
        )


    @pl.when(is_owner)
    def _():
        own = pl.ds(pl.multiple_of(8 * mine, 8), 8)
        slots[me] = gram[own, :]

        def take(i, carry):
            source = lax.rem(me + i, devices)
            pltpu.make_async_remote_copy(
                src_ref=gram.at[pl.ds(0, 8)], dst_ref=slots.at[source],
                send_sem=rs_send.at[0], recv_sem=rs_recv.at[source],
                device_id=device(source), device_id_type=MESH,
            ).wait_recv()
            return carry

        lax.fori_loop(1, devices, take, 0)
        red[...] = jnp.sum(slots[...], axis=0) * (1.0 / (cells * samples * devices))
        total[own, :] = red[...]

        def give(i, carry):
            gather(i).start()
            return carry

        lax.fori_loop(1, devices, give, 0)

        def given(i, carry):
            gather(i).wait_send()
            return carry

        lax.fori_loop(1, devices, given, 0)

    def get(j, carry):
        @pl.when(j * step != me)
        def _():
            pltpu.make_async_remote_copy(
                src_ref=red, dst_ref=total.at[pl.ds(8 * j, 8)],
                send_sem=ag_send.at[0], recv_sem=ag_recv.at[j],
                device_id=device(j * step), device_id_type=MESH,
            ).wait_recv()

        return carry

    lax.fori_loop(0, owners, get, 0)
    lax.fori_loop(0, owners, end_scatter, 0)
    gram_o[...] = total[...]
    out.wait()
    keep.wait()


def eliminate(gram, width=4):
    n = gram.shape[0]
    row = lax.broadcasted_iota(jnp.int32, (n, n), 0)
    col = lax.broadcasted_iota(jnp.int32, (n, n), 1)
    a, w = gram, (row == col).astype(F32)
    for k in range(0, n, width):
        cols, rows_a, rows_w = [], [], []
        low = k // 8 * 8
        for j in range(k, k + width):
            c = jnp.broadcast_to(a[low:, j : j + 1], (n - low, n))
            ra, rw = a[j : j + 1, :], w[j : j + 1, :]
            for i in range(len(cols)):
                factor = cols[i][j - low : j - low + 1, :]
                c = c - cols[i] * factor
                ra = ra - rows_a[i] * factor
                rw = rw - rows_w[i] * factor
            scale = lax.rsqrt(c[j - low : j - low + 1, :])
            cols.append(c * scale)
            rows_a.append(ra * scale)
            rows_w.append(rw * scale)
        below = row[low:] >= k + width
        ta, tw = a[low:], w[low:]
        for j in range(width):
            c = jnp.where(below, cols[j], 0.0)
            here = row[low:] == k + j
            ta = jnp.where(here, rows_a[j], ta - c * rows_a[j])
            tw = jnp.where(here, rows_w[j], tw - c * rows_w[j])
        a = ta if low == 0 else jnp.concatenate([a[:low], ta], axis=0)
        w = tw if low == 0 else jnp.concatenate([w[:low], tw], axis=0)
    return jnp.where(col >= row, a, 0.0), jnp.where(col <= row, w, 0.0)


def orthogonalize(gram, s, second, factor_o, basis_o, next_o, s_v, out, sem, out_sem):
    snaps = gram.shape[0]
    keep = pltpu.make_async_copy(second, next_o, sem.at[0])
    keep.start()
    get = pltpu.make_async_copy(s, s_v, sem.at[1])
    get.start()
    factor, inverse = eliminate(gram[...])
    factor_o[...] = factor
    hi, low = split(inverse)
    both = jnp.concatenate([jnp.concatenate([hi, hi], axis=1), jnp.concatenate([low, low], axis=1)], axis=0)
    get.wait()
    per_x = basis_o.shape[2]

    def layer(x):
        return pltpu.make_async_copy(out.at[x], basis_o.at[:, x], out_sem.at[x])

    def body(x, carry):
        target = out.at[x].reshape(snaps * per_x, out.shape[3])
        for p in range(per_x // 2):
            got = dot(both, s_v[x * (per_x // 2) + p], (1, 0))
            got = got[:snaps] + got[snaps:]
            n = got.shape[1] // 2
            target[pl.ds(2 * p, snaps, stride=per_x), :] = got[:, :n]
            target[pl.ds(2 * p + 1, snaps, stride=per_x), :] = got[:, n:]
        layer(x).start()
        return carry

    lax.fori_loop(0, out.shape[0], body, 0)
    for x in range(out.shape[0]):
        layer(x).wait()
    keep.wait()


def body(nx, ny, field, kappa, history):
    size_x, size_y, depth = field.shape
    past, cells_x, cells_y, samples = history.shape
    cells = cells_x * cells_y
    snaps = past + 2
    owners = snaps // 8
    devices = nx * ny
    anywhere = pl.BlockSpec(memory_space=pl.ANY)
    vmem = pl.BlockSpec(memory_space=pltpu.VMEM)
    padded = pltpu.VMEM((size_x + 2, size_y + 2 * TOP, depth), F32)
    stacked = (cells // 2, 2 * snaps, 2 * samples)
    dma = pltpu.SemaphoreType.DMA
    second, s, gram = pl.pallas_call(
        functools.partial(evolve, nx, ny, past),
        out_shape=[
            jax.ShapeDtypeStruct(field.shape, F32),
            jax.ShapeDtypeStruct(stacked, BF16),
            jax.ShapeDtypeStruct((snaps, snaps), F32),
        ],
        in_specs=[anywhere] * 3,
        out_specs=[anywhere, anywhere, vmem],
        scratch_shapes=[
            padded, padded, padded,
            pltpu.VMEM((snaps * cells, samples), F32),
            pltpu.VMEM(stacked, BF16),
            pltpu.VMEM((snaps, snaps), F32),
            pltpu.VMEM((devices, 8, snaps), F32),
            pltpu.VMEM((8, snaps), F32),
            pltpu.VMEM((snaps, snaps), F32),
            dma((3,)), dma((3, 4)), dma((3, 4)),
            dma((owners,)), dma((devices,)), dma((devices,)), dma((owners,)),
        ],
        compiler_params=pltpu.CompilerParams(
            collective_id=0, has_side_effects=True, vmem_limit_bytes=48 << 20
        ),
        name="evolve",
    )(field, kappa, history.reshape(past * cells, samples))
    factor, basis, field_next = pl.pallas_call(
        orthogonalize,
        out_shape=[
            jax.ShapeDtypeStruct((snaps, snaps), F32),
            jax.ShapeDtypeStruct((snaps, cells_x, cells_y, samples), F32),
            jax.ShapeDtypeStruct(field.shape, F32),
        ],
        in_specs=[vmem, anywhere, anywhere],
        out_specs=[vmem, anywhere, anywhere],
        scratch_shapes=[
            pltpu.VMEM(stacked, BF16),
            pltpu.VMEM((cells_x, snaps, cells_y, samples), F32),
            dma((2,)), dma((cells_x,)),
        ],
        compiler_params=pltpu.CompilerParams(vmem_limit_bytes=48 << 20),
        name="orthogonalize",
    )(gram, s, second)
    return field_next, basis, factor


def solution(mesh):
    placed = (P("gx", "gy", None), P("gx", "gy", None), P(None, "gx", "gy", None))
    return jax.shard_map(
        functools.partial(body, mesh.shape["gx"], mesh.shape["gy"]),
        mesh=mesh,
        in_specs=placed,
        out_specs=(P("gx", "gy", None), P(None, "gx", "gy", None), P()),
        check_vma=False,
    )
```

```python
import functools

import jax
import jax.numpy as jnp
from jax import lax
from jax.experimental import pallas as pl
from jax.experimental.pallas import tpu as pltpu
from jax.sharding import PartitionSpec as P

F32 = jnp.float32
BF16 = jnp.bfloat16
TOP = 8
MESH = pl.DeviceIdType.MESH


def dot(a, b, contract):
    return lax.dot_general(
        a, b, ((contract[:1], contract[1:]), ((), ())), preferred_element_type=F32
    )


def split(x):
    hi = x.astype(BF16)
    return hi, (x - hi.astype(F32)).astype(BF16)


def stencil(v, k, out, tiles):
    size_x = v.shape[0] - 2
    depth = v.shape[2]
    lane = lax.broadcasted_iota(jnp.int32, (8, depth), 1)

    for tile in tiles:
        at = TOP + 8 * tile
        rows = pl.ds(at, 8)
        up = pl.ds(at + 1, 8)
        down = pl.ds(at - 1, 8)

        def layer(x, flux):
            c, kc = v[x, rows, :], k[x, rows, :]
            ahead = (kc + k[x + 1, rows, :]) * (v[x + 1, rows, :] - c)
            acc = ahead - flux
            acc += (kc + k[x, up, :]) * (v[x, up, :] - c)
            acc += (kc + k[x, down, :]) * (v[x, down, :] - c)
            last = lane == depth - 1
            c_up = jnp.where(last, 0.0, pltpu.roll(c, depth - 1, 1))
            k_up = jnp.where(last, 0.0, pltpu.roll(kc, depth - 1, 1))
            acc += (kc + k_up) * (c_up - c)
            c_down = jnp.where(lane == 0, 0.0, pltpu.roll(c, 1, 1))
            k_down = jnp.where(lane == 0, 0.0, pltpu.roll(kc, 1, 1))
            acc += (kc + k_down) * (c_down - c)
            out[x, rows, :] = c + 0.5 * acc
            return ahead

        first = (k[0, rows, :] + k[1, rows, :]) * (v[1, rows, :] - v[0, rows, :])
        lax.fori_loop(1, size_x + 1, layer, first, unroll=4)


def sample(v, pick, rows_y):
    parts = []
    for x in range(1, v.shape[0] - 1, 2):
        parts += [v[x, pl.ds(TOP + 4 * y, 1), :] for y in range(rows_y)]
    x = jnp.concatenate(parts, axis=0)
    hi = x.astype(BF16)
    rest = x - hi.astype(F32)
    mid = rest.astype(BF16)
    low = (rest - mid.astype(F32)).astype(BF16)
    n = x.shape[0]
    got = dot(jnp.concatenate([hi, mid, low], axis=0), pick, (1, 0))
    return got[:n] + got[n : 2 * n] + got[2 * n :]


def evolve(
    nx, ny, past, field, kappa, hist, second_o, s_o, gram_o,
    f, k, v, block, s, gram, slots, red, total, ends,
    load, halo_send, halo_recv, rs_send, rs_recv, ag_send, ag_recv, end_send, end_recv,
):
    size_x, size_y, depth = field.shape
    gx, gy = lax.axis_index("gx"), lax.axis_index("gy")
    devices = nx * ny
    snaps = gram.shape[0]
    owners = snaps // 8
    step = devices // owners
    me = gy * nx + gx

    def device(flat):
        return (lax.rem(flat, nx), lax.div(flat, nx))

    barrier = pltpu.get_barrier_semaphore()

    def greet(i, carry):
        pl.semaphore_signal(barrier, inc=1, device_id=device(lax.rem(me + i, devices)), device_id_type=MESH)
        return carry

    lax.fori_loop(1, devices, greet, 0)

    inner = (pl.ds(1, size_x), pl.ds(TOP, size_y))
    loads = [
        pltpu.make_async_copy(field, f.at[inner], load.at[0]),
        pltpu.make_async_copy(kappa, k.at[inner], load.at[1]),
        pltpu.make_async_copy(hist, block.at[pl.ds(0, hist.shape[0])], load.at[2]),
    ]
    for copy in loads:
        copy.start()

    left, right = gx > 0, gx < nx - 1
    below, above = gy > 0, gy < ny - 1
    whole_y = pl.ds(TOP, size_y)
    whole_x = pl.ds(1, size_x)
    sides = [
        (left, right, (gx - 1, gy), (1, whole_y), (size_x + 1, whole_y)),
        (right, left, (gx + 1, gy), (size_x, whole_y), (0, whole_y)),
        (below, above, (gx, gy - 1), (whole_x, pl.ds(TOP, 1)), (whole_x, pl.ds(TOP + size_y, 1))),
        (above, below, (gx, gy + 1), (whole_x, pl.ds(TOP + size_y - 1, 1)), (whole_x, pl.ds(TOP - 1, 1))),
    ]

    def halo(ref, which, side):
        to, _, place, src, dst = sides[side]
        return pltpu.make_async_remote_copy(
            src_ref=ref.at[src], dst_ref=ref.at[dst],
            send_sem=halo_send.at[which, side], recv_sem=halo_recv.at[which, side],
            device_id=place, device_id_type=MESH,
        )

    def exchange(ref, which, order):
        for side in order:
            pl.when(sides[side][0])(halo(ref, which, side).start)

    def arrive(ref, which):
        for side in range(4):
            pl.when(sides[side][1])(halo(ref, which, side).wait_recv)

    def sent(ref, which):
        for side in range(4):
            pl.when(sides[side][0])(halo(ref, which, side).wait_send)

    for ref in (f, k, v):
        for side in range(4):
            dst = sides[side][4]

            @pl.when(jnp.logical_not(sides[side][1]))
            def _(ref=ref, dst=dst, side=side):
                if side < 2:
                    ref[dst[0], dst[1], :] = jnp.zeros((size_y, depth), F32)
                else:
                    for x in range(size_x):
                        ref[x + 1, dst[1], :] = jnp.zeros((1, depth), F32)

    pl.semaphore_wait(barrier, devices - 1)
    loads[0].wait()
    exchange(f, 0, range(4))
    loads[1].wait()
    exchange(k, 1, range(4))

    samples = depth // 12
    pick = (
        lax.broadcasted_iota(jnp.int32, (depth, samples), 0)
        == 12 * lax.broadcasted_iota(jnp.int32, (depth, samples), 1)
    ).astype(F32).astype(BF16)

    loads[2].wait()
    cells = hist.shape[0] // past
    block[pl.ds(past * cells, 2 * cells), :] = jnp.zeros((2 * cells, samples), F32)

    def pair(p, acc):
        x = jnp.concatenate(
            [block[pl.ds(2 * p, snaps, stride=cells), :], block[pl.ds(2 * p + 1, snaps, stride=cells), :]], axis=1
        )
        both = jnp.concatenate(split(x), axis=0)
        s[p] = both
        return acc + dot(both, both, (1, 1))

    acc = lax.fori_loop(0, cells // 2, pair, jnp.zeros((2 * snaps, 2 * snaps), F32), unroll=2)
    gram[...] = (acc[:snaps, :snaps] + acc[snaps:, snaps:]) + (acc[:snaps, snaps:] + acc[snaps:, :snaps])

    is_owner = (lax.rem(me, step) == 0) & (me < (owners - 1) * step)
    mine = lax.div(me, step)

    def scatter(j):
        return pltpu.make_async_remote_copy(
            src_ref=gram.at[pl.ds(8 * j, 8)], dst_ref=slots.at[me],
            send_sem=rs_send.at[j], recv_sem=rs_recv.at[me],
            device_id=device(j * step), device_id_type=MESH,
        )

    def start_scatter(j, carry):
        pl.when(j * step != me)(lambda: scatter(j).start())
        return carry

    def end_scatter(j, carry):
        pl.when(j * step != me)(lambda: scatter(j).wait_send())
        return carry


    def gather(i):
        to = lax.rem(me + i, devices)
        return pltpu.make_async_remote_copy(
            src_ref=red, dst_ref=total.at[pl.ds(8 * mine, 8)],
            send_sem=ag_send.at[i], recv_sem=ag_recv.at[mine],
            device_id=device(to), device_id_type=MESH,
        )


    lax.fori_loop(0, owners - 1, start_scatter, 0)
    arrive(f, 0)
    arrive(k, 1)
    tiles = size_y // 8
    edge = sorted({0, tiles - 1})
    middle = [t for t in range(tiles) if t not in edge]
    stencil(f, k, v, edge)
    exchange(v, 2, (2, 3))
    stencil(f, k, v, middle)
    exchange(v, 2, (0, 1))

    @pl.when(is_owner)
    def _():
        own = pl.ds(pl.multiple_of(8 * mine, 8), 8)
        slots[me] = gram[own, :]

        def take(i, carry):
            source = lax.rem(me + i, devices)
            pltpu.make_async_remote_copy(
                src_ref=gram.at[pl.ds(0, 8)], dst_ref=slots.at[source],
                send_sem=rs_send.at[0], recv_sem=rs_recv.at[source],
                device_id=device(source), device_id_type=MESH,
            ).wait_recv()
            return carry

        lax.fori_loop(1, devices, take, 0)
        red[...] = jnp.sum(slots[...], axis=0) * (1.0 / (cells * samples * devices))
        total[own, :] = red[...]

        def give(i, carry):
            gather(i).start()
            return carry

        lax.fori_loop(1, devices, give, 0)

    block[pl.ds(past * cells, cells), :] = sample(v, pick, size_y // 4)
    sent(f, 0)
    sent(k, 1)
    arrive(v, 2)
    stencil(v, k, f, range(tiles))
    out = pltpu.make_async_copy(f.at[inner], second_o, load.at[0])
    out.start()
    block[pl.ds((past + 1) * cells, cells), :] = sample(f, pick, size_y // 4)
    sent(v, 2)

    def tail(p, acc):
        x = jnp.concatenate(
            [
                block[pl.ds((snaps - 16) * cells + 2 * p, 16, stride=cells), :],
                block[pl.ds((snaps - 16) * cells + 2 * p + 1, 16, stride=cells), :],
            ],
            axis=1,
        )
        hi, low = split(x)
        s[p, pl.ds(snaps - 16, 16), :] = hi
        s[p, pl.ds(2 * snaps - 16, 16), :] = low
        return acc + dot(jnp.concatenate([hi, low], axis=0), s[p], (1, 1))

    acc = lax.fori_loop(0, cells // 2, tail, jnp.zeros((32, 2 * snaps), F32), unroll=4)
    acc = acc[8:16] + acc[24:]
    ends[me] = acc[:, :snaps] + acc[:, snaps:]
    keep = pltpu.make_async_copy(s, s_o, load.at[1])
    keep.start()

    def swap(i, source):
        return pltpu.make_async_remote_copy(
            src_ref=ends.at[me], dst_ref=ends.at[source],
            send_sem=end_send.at[i], recv_sem=end_recv.at[source],
            device_id=device(lax.rem(me + i, devices)), device_id_type=MESH,
        )

    def start_swap(i, carry):
        swap(i, me).start()
        return carry

    def end_swap(i, carry):
        swap(i, lax.rem(me + i, devices)).wait_recv()
        return carry

    def sent_swap(i, carry):
        swap(i, me).wait_send()
        return carry

    lax.fori_loop(1, devices, start_swap, 0)

    @pl.when(is_owner)
    def _():
        def given(i, carry):
            gather(i).wait_send()
            return carry

        lax.fori_loop(1, devices, given, 0)

    def get(j, carry):
        @pl.when(j * step != me)
        def _():
            pltpu.make_async_remote_copy(
                src_ref=red, dst_ref=total.at[pl.ds(8 * j, 8)],
                send_sem=ag_send.at[0], recv_sem=ag_recv.at[j],
                device_id=device(j * step), device_id_type=MESH,
            ).wait_recv()

        return carry

    lax.fori_loop(0, owners - 1, get, 0)
    lax.fori_loop(0, owners - 1, end_scatter, 0)
    lax.fori_loop(1, devices, end_swap, 0)
    total[pl.ds(snaps - 8, 8), :] = jnp.sum(ends[...], axis=0) * (1.0 / (cells * samples * devices))
    lax.fori_loop(1, devices, sent_swap, 0)
    gram_o[...] = total[...]
    out.wait()
    keep.wait()


def eliminate(gram, width=4):
    n = gram.shape[0]
    row = lax.broadcasted_iota(jnp.int32, (n, n), 0)
    col = lax.broadcasted_iota(jnp.int32, (n, n), 1)
    a, w = gram, (row == col).astype(F32)
    for k in range(0, n, width):
        cols, rows_a, rows_w = [], [], []
        low = k // 8 * 8
        for j in range(k, k + width):
            c = jnp.broadcast_to(a[low:, j : j + 1], (n - low, n))
            ra, rw = a[j : j + 1, :], w[j : j + 1, :]
            for i in range(len(cols)):
                factor = cols[i][j - low : j - low + 1, :]
                c = c - cols[i] * factor
                ra = ra - rows_a[i] * factor
                rw = rw - rows_w[i] * factor
            scale = lax.rsqrt(c[j - low : j - low + 1, :])
            cols.append(c * scale)
            rows_a.append(ra * scale)
            rows_w.append(rw * scale)
        below = row[low:] >= k + width
        ta, tw = a[low:], w[low:]
        for j in range(width):
            c = jnp.where(below, cols[j], 0.0)
            here = row[low:] == k + j
            ta = jnp.where(here, rows_a[j], ta - c * rows_a[j])
            tw = jnp.where(here, rows_w[j], tw - c * rows_w[j])
        a = ta if low == 0 else jnp.concatenate([a[:low], ta], axis=0)
        w = tw if low == 0 else jnp.concatenate([w[:low], tw], axis=0)
    return jnp.where(col >= row, a, 0.0), jnp.where(col <= row, w, 0.0)


def orthogonalize(gram, s, second, factor_o, basis_o, next_o, s_v, out, sem, out_sem):
    snaps = gram.shape[0]
    keep = pltpu.make_async_copy(second, next_o, sem.at[0])
    keep.start()
    get = pltpu.make_async_copy(s, s_v, sem.at[1])
    get.start()
    row = lax.broadcasted_iota(jnp.int32, (snaps, snaps), 0)
    col = lax.broadcasted_iota(jnp.int32, (snaps, snaps), 1)
    factor, inverse = eliminate(jnp.where(col <= row, gram[...], gram[...].T))
    factor_o[...] = factor
    hi, low = split(inverse)
    both = jnp.concatenate([jnp.concatenate([hi, hi], axis=1), jnp.concatenate([low, low], axis=1)], axis=0)
    get.wait()
    per_x = basis_o.shape[2]

    def layer(x):
        return pltpu.make_async_copy(out.at[x], basis_o.at[:, x], out_sem.at[x])

    def body(x, carry):
        target = out.at[x].reshape(snaps * per_x, out.shape[3])
        for p in range(per_x // 2):
            got = dot(both, s_v[x * (per_x // 2) + p], (1, 0))
            got = got[:snaps] + got[snaps:]
            n = got.shape[1] // 2
            target[pl.ds(2 * p, snaps, stride=per_x), :] = got[:, :n]
            target[pl.ds(2 * p + 1, snaps, stride=per_x), :] = got[:, n:]
        layer(x).start()
        return carry

    lax.fori_loop(0, out.shape[0], body, 0)
    for x in range(out.shape[0]):
        layer(x).wait()
    keep.wait()


def body(nx, ny, field, kappa, history):
    size_x, size_y, depth = field.shape
    past, cells_x, cells_y, samples = history.shape
    cells = cells_x * cells_y
    snaps = past + 2
    owners = snaps // 8
    devices = nx * ny
    anywhere = pl.BlockSpec(memory_space=pl.ANY)
    vmem = pl.BlockSpec(memory_space=pltpu.VMEM)
    padded = pltpu.VMEM((size_x + 2, size_y + 2 * TOP, depth), F32)
    stacked = (cells // 2, 2 * snaps, 2 * samples)
    dma = pltpu.SemaphoreType.DMA
    second, s, gram = pl.pallas_call(
        functools.partial(evolve, nx, ny, past),
        out_shape=[
            jax.ShapeDtypeStruct(field.shape, F32),
            jax.ShapeDtypeStruct(stacked, BF16),
            jax.ShapeDtypeStruct((snaps, snaps), F32),
        ],
        in_specs=[anywhere] * 3,
        out_specs=[anywhere, anywhere, vmem],
        scratch_shapes=[
            padded, padded, padded,
            pltpu.VMEM((snaps * cells, samples), F32),
            pltpu.VMEM(stacked, BF16),
            pltpu.VMEM((snaps, snaps), F32),
            pltpu.VMEM((devices, 8, snaps), F32),
            pltpu.VMEM((8, snaps), F32),
            pltpu.VMEM((snaps, snaps), F32),
            pltpu.VMEM((devices, 8, snaps), F32),
            dma((3,)), dma((3, 4)), dma((3, 4)),
            dma((owners,)), dma((devices,)), dma((devices,)), dma((owners,)),
            dma((devices,)), dma((devices,)),
        ],
        compiler_params=pltpu.CompilerParams(
            collective_id=0, has_side_effects=True, vmem_limit_bytes=48 << 20
        ),
        name="evolve",
    )(field, kappa, history.reshape(past * cells, samples))
    factor, basis, field_next = pl.pallas_call(
        orthogonalize,
        out_shape=[
            jax.ShapeDtypeStruct((snaps, snaps), F32),
            jax.ShapeDtypeStruct((snaps, cells_x, cells_y, samples), F32),
            jax.ShapeDtypeStruct(field.shape, F32),
        ],
        in_specs=[vmem, anywhere, anywhere],
        out_specs=[vmem, anywhere, anywhere],
        scratch_shapes=[
            pltpu.VMEM(stacked, BF16),
            pltpu.VMEM((cells_x, snaps, cells_y, samples), F32),
            dma((2,)), dma((cells_x,)),
        ],
        compiler_params=pltpu.CompilerParams(vmem_limit_bytes=48 << 20),
        name="orthogonalize",
    )(gram, s, second)
    return field_next, basis, factor


def solution(mesh):
    placed = (P("gx", "gy", None), P("gx", "gy", None), P(None, "gx", "gy", None))
    return jax.shard_map(
        functools.partial(body, mesh.shape["gx"], mesh.shape["gy"]),
        mesh=mesh,
        in_specs=placed,
        out_specs=(P("gx", "gy", None), P(None, "gx", "gy", None), P()),
        check_vma=False,
    )
```

```python
import functools

import jax
import jax.numpy as jnp
from jax import lax
from jax.experimental import pallas as pl
from jax.experimental.pallas import tpu as pltpu
from jax.sharding import PartitionSpec as P

F32 = jnp.float32
BF16 = jnp.bfloat16
TOP = 8
MESH = pl.DeviceIdType.MESH


def dot(a, b, contract):
    return lax.dot_general(
        a, b, ((contract[:1], contract[1:]), ((), ())), preferred_element_type=F32
    )


def split(x):
    hi = x.astype(BF16)
    return hi, (x - hi.astype(F32)).astype(BF16)


def stencil(v, k, out, tiles, start, stop):
    unroll = next(u for u in (8, 7, 4, 2, 1) if (stop - start) % u == 0)
    depth = v.shape[2]
    lane = lax.broadcasted_iota(jnp.int32, (8, depth), 1)

    for tile in tiles:
        at = TOP + 8 * tile
        rows = pl.ds(at, 8)
        up = pl.ds(at + 1, 8)
        down = pl.ds(at - 1, 8)

        def layer(x, flux):
            c, kc = v[x, rows, :], k[x, rows, :]
            ahead = (kc + k[x + 1, rows, :]) * (v[x + 1, rows, :] - c)
            acc = ahead - flux
            acc += (kc + k[x, up, :]) * (v[x, up, :] - c)
            acc += (kc + k[x, down, :]) * (v[x, down, :] - c)
            last = lane == depth - 1
            c_up = jnp.where(last, 0.0, pltpu.roll(c, depth - 1, 1))
            k_up = jnp.where(last, 0.0, pltpu.roll(kc, depth - 1, 1))
            acc += (kc + k_up) * (c_up - c)
            c_down = jnp.where(lane == 0, 0.0, pltpu.roll(c, 1, 1))
            k_down = jnp.where(lane == 0, 0.0, pltpu.roll(kc, 1, 1))
            acc += (kc + k_down) * (c_down - c)
            out[x, rows, :] = c + 0.5 * acc
            return ahead

        first = (k[start - 1, rows, :] + k[start, rows, :]) * (v[start, rows, :] - v[start - 1, rows, :])
        lax.fori_loop(start, stop, layer, first, unroll=unroll)


def sample(v, pick, rows_y):
    parts = []
    for x in range(1, v.shape[0] - 1, 2):
        parts += [v[x, pl.ds(TOP + 4 * y, 1), :] for y in range(rows_y)]
    x = jnp.concatenate(parts, axis=0)
    hi = x.astype(BF16)
    rest = x - hi.astype(F32)
    mid = rest.astype(BF16)
    low = (rest - mid.astype(F32)).astype(BF16)
    n = x.shape[0]
    got = dot(jnp.concatenate([hi, mid, low], axis=0), pick, (1, 0))
    return got[:n] + got[n : 2 * n] + got[2 * n :]


def evolve(
    nx, ny, past, field, kappa, hist, second_o, s_o, gram_o,
    f, k, v, block, s, gram, slots, red, total, ends,
    load, halo_send, halo_recv, rs_send, rs_recv, ag_send, ag_recv, end_send, end_recv,
):
    size_x, size_y, depth = field.shape
    gx, gy = lax.axis_index("gx"), lax.axis_index("gy")
    devices = nx * ny
    snaps = gram.shape[0]
    owners = snaps // 8
    step = devices // owners
    me = gy * nx + gx

    def device(flat):
        return (lax.rem(flat, nx), lax.div(flat, nx))

    barrier = pltpu.get_barrier_semaphore()

    def greet(i, carry):
        pl.semaphore_signal(barrier, inc=1, device_id=device(lax.rem(me + i, devices)), device_id_type=MESH)
        return carry

    lax.fori_loop(1, devices, greet, 0)

    inner = (pl.ds(1, size_x), pl.ds(TOP, size_y))
    loads = [
        pltpu.make_async_copy(field, f.at[inner], load.at[0]),
        pltpu.make_async_copy(kappa, k.at[inner], load.at[1]),
        pltpu.make_async_copy(hist, block.at[pl.ds(0, hist.shape[0])], load.at[2]),
    ]
    for copy in loads:
        copy.start()

    left, right = gx > 0, gx < nx - 1
    below, above = gy > 0, gy < ny - 1
    whole_y = pl.ds(TOP, size_y)
    whole_x = pl.ds(1, size_x)
    sides = [
        (left, right, (gx - 1, gy), (1, whole_y), (size_x + 1, whole_y)),
        (right, left, (gx + 1, gy), (size_x, whole_y), (0, whole_y)),
        (below, above, (gx, gy - 1), (whole_x, pl.ds(TOP, 1)), (whole_x, pl.ds(TOP + size_y, 1))),
        (above, below, (gx, gy + 1), (whole_x, pl.ds(TOP + size_y - 1, 1)), (whole_x, pl.ds(TOP - 1, 1))),
    ]

    def halo(ref, which, side):
        to, _, place, src, dst = sides[side]
        return pltpu.make_async_remote_copy(
            src_ref=ref.at[src], dst_ref=ref.at[dst],
            send_sem=halo_send.at[which, side], recv_sem=halo_recv.at[which, side],
            device_id=place, device_id_type=MESH,
        )

    def exchange(ref, which, order):
        for side in order:
            pl.when(sides[side][0])(halo(ref, which, side).start)

    def arrive(ref, which):
        for side in range(4):
            pl.when(sides[side][1])(halo(ref, which, side).wait_recv)

    def sent(ref, which):
        for side in range(4):
            pl.when(sides[side][0])(halo(ref, which, side).wait_send)

    for ref in (f, k, v):
        for side in range(4):
            dst = sides[side][4]

            @pl.when(jnp.logical_not(sides[side][1]))
            def _(ref=ref, dst=dst, side=side):
                if side < 2:
                    ref[dst[0], dst[1], :] = jnp.zeros((size_y, depth), F32)
                else:
                    for x in range(size_x):
                        ref[x + 1, dst[1], :] = jnp.zeros((1, depth), F32)

    pl.semaphore_wait(barrier, devices - 1)
    loads[0].wait()
    exchange(f, 0, range(4))
    loads[1].wait()
    exchange(k, 1, range(4))

    samples = depth // 12
    pick = (
        lax.broadcasted_iota(jnp.int32, (depth, samples), 0)
        == 12 * lax.broadcasted_iota(jnp.int32, (depth, samples), 1)
    ).astype(F32).astype(BF16)

    loads[2].wait()
    cells = hist.shape[0] // past
    block[pl.ds(past * cells, 2 * cells), :] = jnp.zeros((2 * cells, samples), F32)

    def group(first, rows, start):
        wide = []
        for p in range(4):
            at = start * cells + 8 * first + 2 * p
            x = jnp.concatenate(
                [block[pl.ds(at, rows, stride=cells), :], block[pl.ds(at + 1, rows, stride=cells), :]], axis=1
            )
            hi, low = split(x)
            s[4 * first + p, pl.ds(start, rows), :] = hi
            s[4 * first + p, pl.ds(snaps + start, rows), :] = low
            wide.append(jnp.concatenate([hi, low], axis=0))
        return jnp.concatenate(wide, axis=1)

    def pair(q, acc):
        both = group(q, snaps, 0)
        return acc + dot(both, both, (1, 1))

    acc = lax.fori_loop(0, cells // 8, pair, jnp.zeros((2 * snaps, 2 * snaps), F32))
    gram[...] = (acc[:snaps, :snaps] + acc[snaps:, snaps:]) + (acc[:snaps, snaps:] + acc[snaps:, :snaps])

    is_owner = (lax.rem(me, step) == 0) & (me < (owners - 1) * step)
    mine = lax.div(me, step)

    def scatter(j):
        return pltpu.make_async_remote_copy(
            src_ref=gram.at[pl.ds(8 * j, 8)], dst_ref=slots.at[me],
            send_sem=rs_send.at[j], recv_sem=rs_recv.at[me],
            device_id=device(j * step), device_id_type=MESH,
        )

    def start_scatter(j, carry):
        pl.when(j * step != me)(lambda: scatter(j).start())
        return carry

    def end_scatter(j, carry):
        pl.when(j * step != me)(lambda: scatter(j).wait_send())
        return carry


    def gather(i):
        to = lax.rem(me + i, devices)
        return pltpu.make_async_remote_copy(
            src_ref=red, dst_ref=total.at[pl.ds(8 * mine, 8)],
            send_sem=ag_send.at[i], recv_sem=ag_recv.at[mine],
            device_id=device(to), device_id_type=MESH,
        )


    lax.fori_loop(0, owners - 1, start_scatter, 0)
    arrive(f, 0)
    arrive(k, 1)
    tiles = size_y // 8
    edge = sorted({0, tiles - 1})
    middle = [t for t in range(tiles) if t not in edge]
    stencil(f, k, v, edge, 1, size_x + 1)
    exchange(v, 2, (2, 3))
    stencil(f, k, v, middle, 1, size_x + 1)
    exchange(v, 2, (0, 1))

    @pl.when(is_owner)
    def _():
        own = pl.ds(pl.multiple_of(8 * mine, 8), 8)
        slots[me] = gram[own, :]

        def take(i, carry):
            source = lax.rem(me + i, devices)
            pltpu.make_async_remote_copy(
                src_ref=gram.at[pl.ds(0, 8)], dst_ref=slots.at[source],
                send_sem=rs_send.at[0], recv_sem=rs_recv.at[source],
                device_id=device(source), device_id_type=MESH,
            ).wait_recv()
            return carry

        lax.fori_loop(1, devices, take, 0)
        red[...] = jnp.sum(slots[...], axis=0) * (1.0 / (cells * samples * devices))
        total[own, :] = red[...]

        def give(i, carry):
            gather(i).start()
            return carry

        lax.fori_loop(1, devices, give, 0)

    block[pl.ds(past * cells, cells), :] = sample(v, pick, size_y // 4)
    sent(f, 0)
    sent(k, 1)
    stencil(v, k, f, middle, 2, size_x)
    arrive(v, 2)
    stencil(v, k, f, edge, 1, size_x + 1)
    stencil(v, k, f, middle, 1, 2)
    stencil(v, k, f, middle, size_x, size_x + 1)
    out = pltpu.make_async_copy(f.at[inner], second_o, load.at[0])
    out.start()
    block[pl.ds((past + 1) * cells, cells), :] = sample(f, pick, size_y // 4)
    sent(v, 2)

    def tail(q, acc):
        both = group(q, 16, snaps - 16)
        all_rows = jnp.concatenate([s[4 * q + p] for p in range(4)], axis=1)
        return acc + dot(both, all_rows, (1, 1))

    acc = lax.fori_loop(0, cells // 8, tail, jnp.zeros((32, 2 * snaps), F32))
    acc = acc[8:16] + acc[24:]
    ends[me] = acc[:, :snaps] + acc[:, snaps:]
    keep = pltpu.make_async_copy(s, s_o, load.at[1])
    keep.start()

    def swap(i, source):
        return pltpu.make_async_remote_copy(
            src_ref=ends.at[me], dst_ref=ends.at[source],
            send_sem=end_send.at[i], recv_sem=end_recv.at[source],
            device_id=device(lax.rem(me + i, devices)), device_id_type=MESH,
        )

    def start_swap(i, carry):
        swap(i, me).start()
        return carry

    def end_swap(i, carry):
        swap(i, lax.rem(me + i, devices)).wait_recv()
        return carry

    def sent_swap(i, carry):
        swap(i, me).wait_send()
        return carry

    lax.fori_loop(1, devices, start_swap, 0)

    @pl.when(is_owner)
    def _():
        def given(i, carry):
            gather(i).wait_send()
            return carry

        lax.fori_loop(1, devices, given, 0)

    def get(j, carry):
        @pl.when(j * step != me)
        def _():
            pltpu.make_async_remote_copy(
                src_ref=red, dst_ref=total.at[pl.ds(8 * j, 8)],
                send_sem=ag_send.at[0], recv_sem=ag_recv.at[j],
                device_id=device(j * step), device_id_type=MESH,
            ).wait_recv()

        return carry

    lax.fori_loop(0, owners - 1, get, 0)
    lax.fori_loop(0, owners - 1, end_scatter, 0)
    lax.fori_loop(1, devices, end_swap, 0)
    total[pl.ds(snaps - 8, 8), :] = jnp.sum(ends[...], axis=0) * (1.0 / (cells * samples * devices))
    lax.fori_loop(1, devices, sent_swap, 0)
    gram_o[...] = total[...]
    out.wait()
    keep.wait()


def eliminate(gram, width=4):
    n = gram.shape[0]
    row = lax.broadcasted_iota(jnp.int32, (n, n), 0)
    col = lax.broadcasted_iota(jnp.int32, (n, n), 1)
    a, w = gram, (row == col).astype(F32)
    for k in range(0, n, width):
        cols, rows_a, rows_w = [], [], []
        low = k // 8 * 8
        for j in range(k, k + width):
            c = jnp.broadcast_to(a[low:, j : j + 1], (n - low, n))
            ra, rw = a[j : j + 1, :], w[j : j + 1, :]
            for i in range(len(cols)):
                factor = cols[i][j - low : j - low + 1, :]
                c = c - cols[i] * factor
                ra = ra - rows_a[i] * factor
                rw = rw - rows_w[i] * factor
            scale = lax.rsqrt(c[j - low : j - low + 1, :])
            cols.append(c * scale)
            rows_a.append(ra * scale)
            rows_w.append(rw * scale)
        below = row[low:] >= k + width
        ta, tw = a[low:], w[low:]
        for j in range(width):
            c = jnp.where(below, cols[j], 0.0)
            here = row[low:] == k + j
            ta = jnp.where(here, rows_a[j], ta - c * rows_a[j])
            tw = jnp.where(here, rows_w[j], tw - c * rows_w[j])
        a = ta if low == 0 else jnp.concatenate([a[:low], ta], axis=0)
        w = tw if low == 0 else jnp.concatenate([w[:low], tw], axis=0)
    return jnp.where(col >= row, a, 0.0), jnp.where(col <= row, w, 0.0)


def orthogonalize(gram, s, second, factor_o, basis_o, next_o, s_v, out, sem, out_sem):
    snaps = gram.shape[0]
    keep = pltpu.make_async_copy(second, next_o, sem.at[0])
    keep.start()
    get = pltpu.make_async_copy(s, s_v, sem.at[1])
    get.start()
    row = lax.broadcasted_iota(jnp.int32, (snaps, snaps), 0)
    col = lax.broadcasted_iota(jnp.int32, (snaps, snaps), 1)
    factor, inverse = eliminate(jnp.where(col <= row, gram[...], gram[...].T))
    factor_o[...] = factor
    hi, low = split(inverse)
    both = jnp.concatenate([jnp.concatenate([hi, hi], axis=1), jnp.concatenate([low, low], axis=1)], axis=0)
    get.wait()
    per_x = basis_o.shape[2]

    def layer(x):
        return pltpu.make_async_copy(out.at[x], basis_o.at[:, x], out_sem.at[x])

    def body(x, carry):
        target = out.at[x].reshape(snaps * per_x, out.shape[3])
        for p in range(per_x // 2):
            got = dot(both, s_v[x * (per_x // 2) + p], (1, 0))
            got = got[:snaps] + got[snaps:]
            n = got.shape[1] // 2
            target[pl.ds(2 * p, snaps, stride=per_x), :] = got[:, :n]
            target[pl.ds(2 * p + 1, snaps, stride=per_x), :] = got[:, n:]
        layer(x).start()
        return carry

    lax.fori_loop(0, out.shape[0], body, 0)
    for x in range(out.shape[0]):
        layer(x).wait()
    keep.wait()


def body(nx, ny, field, kappa, history):
    size_x, size_y, depth = field.shape
    past, cells_x, cells_y, samples = history.shape
    cells = cells_x * cells_y
    snaps = past + 2
    owners = snaps // 8
    devices = nx * ny
    anywhere = pl.BlockSpec(memory_space=pl.ANY)
    vmem = pl.BlockSpec(memory_space=pltpu.VMEM)
    padded = pltpu.VMEM((size_x + 2, size_y + 2 * TOP, depth), F32)
    stacked = (cells // 2, 2 * snaps, 2 * samples)
    dma = pltpu.SemaphoreType.DMA
    second, s, gram = pl.pallas_call(
        functools.partial(evolve, nx, ny, past),
        out_shape=[
            jax.ShapeDtypeStruct(field.shape, F32),
            jax.ShapeDtypeStruct(stacked, BF16),
            jax.ShapeDtypeStruct((snaps, snaps), F32),
        ],
        in_specs=[anywhere] * 3,
        out_specs=[anywhere, anywhere, vmem],
        scratch_shapes=[
            padded, padded, padded,
            pltpu.VMEM((snaps * cells, samples), F32),
            pltpu.VMEM(stacked, BF16),
            pltpu.VMEM((snaps, snaps), F32),
            pltpu.VMEM((devices, 8, snaps), F32),
            pltpu.VMEM((8, snaps), F32),
            pltpu.VMEM((snaps, snaps), F32),
            pltpu.VMEM((devices, 8, snaps), F32),
            dma((3,)), dma((3, 4)), dma((3, 4)),
            dma((owners,)), dma((devices,)), dma((devices,)), dma((owners,)),
            dma((devices,)), dma((devices,)),
        ],
        compiler_params=pltpu.CompilerParams(
            collective_id=0, has_side_effects=True, vmem_limit_bytes=48 << 20
        ),
        name="evolve",
    )(field, kappa, history.reshape(past * cells, samples))
    factor, basis, field_next = pl.pallas_call(
        orthogonalize,
        out_shape=[
            jax.ShapeDtypeStruct((snaps, snaps), F32),
            jax.ShapeDtypeStruct((snaps, cells_x, cells_y, samples), F32),
            jax.ShapeDtypeStruct(field.shape, F32),
        ],
        in_specs=[vmem, anywhere, anywhere],
        out_specs=[vmem, anywhere, anywhere],
        scratch_shapes=[
            pltpu.VMEM(stacked, BF16),
            pltpu.VMEM((cells_x, snaps, cells_y, samples), F32),
            dma((2,)), dma((cells_x,)),
        ],
        compiler_params=pltpu.CompilerParams(vmem_limit_bytes=48 << 20),
        name="orthogonalize",
    )(gram, s, second)
    return field_next, basis, factor


def solution(mesh):
    placed = (P("gx", "gy", None), P("gx", "gy", None), P(None, "gx", "gy", None))
    return jax.shard_map(
        functools.partial(body, mesh.shape["gx"], mesh.shape["gy"]),
        mesh=mesh,
        in_specs=placed,
        out_specs=(P("gx", "gy", None), P(None, "gx", "gy", None), P()),
        check_vma=False,
    )
```
